256 devices in a mesh: bx: 16 (over y, x), by: 16 (over z, core).
Axes of the slice: x: 4, y: 4, z: 8, core: 2. Of those that a mesh axis runs over, the one named last changes fastest.
Arguments:
- coefficients: float32 [16, 16, 2, 64, 2048], P('bx', 'by'), may hold values from -1.5 to 1.5
Outputs:
- transformed: float32 [16, 16, 2, 64, 2048], P('bx', 'by')
The draws below stay inside these ranges and needn't reach their ends.
All inputs are finite; a program needn't handle non-finite values.
Results may differ from the reference program's by a relative error of at most 0.0006.
Values sent between devices are 32-bit elements; how exact they have to be, the bound alone decides.
A program may use at most 64 MiB of HBM per device.

```python
import math
import jax
import jax.numpy as jnp
from jax import lax

SPAT_DEV = 32
CHEB_POINTS = 64
PAIRS_DEV = 2048
N_BX = 16
N_BY = 16


def level_of(own_key, extent, pieces, smallest, top_value):
    def one(axis_at, shards_of):
        heights = jax.random.uniform(jax.random.fold_in(jax.random.fold_in(own_key, 6), axis_at), (shards_of,), jnp.float32, smallest / len(pieces), top_value / len(pieces))
        return jnp.repeat(jnp.exp(heights), extent[axis_at] // shards_of).reshape((-1,) + (1,) * (len(extent) - axis_at - 1))

    factor_of = one(*pieces[0])
    for cut in pieces[1:]:
        factor_of = factor_of * one(*cut)
    return factor_of


def centred(rng, extent, deviation, limit, split=(), held_as=jnp.bfloat16):
    loudness = level_of(rng, extent, split, -0.22, 0.18) if split else 1.0
    array = jax.random.normal(rng, extent, jnp.float32) * deviation * loudness
    return jnp.minimum(jnp.maximum(array, -limit), limit).astype(held_as)


def setup_inputs(seed: int = 0) -> dict:
    arg_keys = jax.random.split(jax.random.key(seed), 2)
    return {
        "coefficients": centred(arg_keys[0], (N_BX, N_BY, 2, CHEB_POINTS, PAIRS_DEV), 0.25, 1.5, ((0, 16), (1, 16)), jnp.float32),
    }


TWO_PI = 2.0 * math.pi

def cheb_points():
    order_index = jnp.arange(4, dtype=jnp.int32).astype(jnp.float32)
    return 0.5 * jnp.cos((2.0 * order_index + 1.0) * (math.pi / 8.0))

def child_weights(child_bit):
    nodes_all = cheb_points()
    targets = (child_bit - 0.5) * 0.5 + 0.5 * nodes_all
    identity = jnp.eye(4, dtype=jnp.float32)
    numer = targets[None, None, :] - nodes_all[None, :, None]
    denom = nodes_all[:, None, None] - nodes_all[None, :, None] + identity[:, :, None]
    factor = jnp.where(identity[:, :, None] > 0.5, jnp.ones_like(numer), numer / denom)
    return jnp.prod(factor, axis=1)

def side_weights(bit_value):
    return jnp.where(bit_value == 1, child_weights(1), child_weights(0))

def cube_matrix(bit_first, bit_second, bit_third):
    joined = jnp.einsum('ad,be,cf->abcdef', side_weights(bit_first), side_weights(bit_second), side_weights(bit_third), precision=lax.Precision.HIGHEST, preferred_element_type=jnp.float32)
    return joined.reshape(64, 64)

def bit_at(value, level_index):
    return value // 2 ** level_index % 2

def partner(value, level_index):
    return value + (1 - 2 * bit_at(value, level_index)) * 2 ** level_index

def logical_index(value, count):
    quarter = count // 4
    upper = value // quarter
    return 4 * (value % quarter) + 2 * (upper % 2) + upper // 2

def physical_index(value, count):
    quarter = count // 4
    return value // 4 + quarter * (2 * (value % 2) + value // 2 % 2)

def low_bits(value, level_index):
    if level_index == 0:
        return 0
    if level_index == 1:
        return value % 2
    return 2 * (value % 2) + value // 2 % 2

def phase_angle(x_first, x_second, x_third, p_first, p_second, p_third):
    radius = jnp.sqrt(p_first * p_first + p_second * p_second + p_third * p_third)
    speed = 0.05 * (1.0 + 0.5 * jnp.sin(TWO_PI * x_first) * jnp.sin(TWO_PI * x_second) + 0.3 * jnp.cos(TWO_PI * x_third))
    return TWO_PI * (x_first * p_first + x_second * p_second + x_third * p_third + speed * radius)

def centers(target_row, target_col, level_index, spatial, n_by):
    zc_count = 2 ** level_index
    cell_size = 0.5 ** (4 + level_index)
    group = target_row // 4 * (n_by // 4) + target_col // 4
    parent = group * spatial + jnp.arange(spatial, dtype=jnp.int32)
    cell_x = 2 * (parent // 64 * zc_count + low_bits(target_row, level_index)) + bit_at(target_row, level_index)
    cell_y = 2 * (parent // 8 % 8 * zc_count + low_bits(target_col, level_index)) + bit_at(target_col, level_index)
    cell_z = 2 * (parent[:, None] % 8 * zc_count + jnp.arange(zc_count, dtype=jnp.int32)[None, :])
    cell_z = cell_z[:, :, None] + jnp.arange(2, dtype=jnp.int32)[None, None, :]
    first = ((cell_x.astype(jnp.float32) + 0.5) * cell_size).reshape(1, spatial, 1, 1, 1, 1, 1)
    second = ((cell_y.astype(jnp.float32) + 0.5) * cell_size).reshape(1, spatial, 1, 1, 1, 1, 1)
    third = ((cell_z.astype(jnp.float32) + 0.5) * cell_size).reshape(1, spatial, 1, 1, zc_count, 2, 1)
    return (first, second, third)

def point_nodes():
    nodes_all = cheb_points()
    point_index = jnp.arange(64, dtype=jnp.int32)
    return (nodes_all[point_index // 16], nodes_all[point_index // 4 % 4], nodes_all[point_index % 4])

def contribute(coeff_block, source_row, source_col, target_row, target_col, level_index, n_by):
    spatial = coeff_block.shape[2]
    zc_count = 2 ** level_index
    half_count = 8 // zc_count
    box_width = 32.0 * zc_count
    node_first, node_second, node_third = point_nodes()
    first, second, third = centers(target_row, target_col, level_index, spatial, n_by)
    side_index = jnp.arange(2, dtype=jnp.int32)
    freq_x = ((4 * side_index + source_row % 4) // zc_count).astype(jnp.float32)
    freq_y = ((4 * side_index + source_col % 4) // zc_count).astype(jnp.float32)
    freq_z = (2 * jnp.arange(half_count, dtype=jnp.int32)[:, None] + side_index[None, :]).astype(jnp.float32)
    p_first = (-256.0 + box_width * (freq_x[None, :] + 0.5 + node_first[:, None])).reshape(64, 1, 2, 1, 1, 1, 1, 1)
    p_second = (-256.0 + box_width * (freq_y[None, :] + 0.5 + node_second[:, None])).reshape(64, 1, 1, 2, 1, 1, 1, 1)
    p_third = (-256.0 + box_width * (freq_z[None] + 0.5 + node_third[:, None, None])).reshape(64, 1, 1, 1, 1, 1, half_count, 2)
    angles = phase_angle(first[..., None], second[..., None], third[..., None], p_first, p_second, p_third)
    cosines = jnp.cos(angles)
    sine_part = jnp.sin(angles)
    shaped = coeff_block.reshape(2, 64, spatial, 2, 2, zc_count, 1, half_count, 2)
    turned = jnp.stack([shaped[0] * cosines - shaped[1] * sine_part, shaped[0] * sine_part + shaped[1] * cosines])
    weights_stack = jnp.stack([cube_matrix(bit_at(source_row, level_index), bit_at(source_col, level_index), 0), cube_matrix(bit_at(source_row, level_index), bit_at(source_col, level_index), 1)], axis=2)
    return jnp.einsum('tsz,rsabcdefz->rtabcdef', weights_stack, turned, precision=lax.Precision.HIGHEST, preferred_element_type=jnp.float32)

def finish(summed, target_row, target_col, level_index, n_by):
    spatial = summed.shape[2]
    zc_count = 2 ** level_index
    half_count = 8 // zc_count
    box_width = 64.0 * zc_count
    node_first, node_second, node_third = point_nodes()
    first, second, third = centers(target_row, target_col, level_index, spatial, n_by)
    side_index = jnp.arange(2, dtype=jnp.int32)
    freq_x = ((4 * side_index + target_row % 4) // (2 * zc_count)).astype(jnp.float32)
    freq_y = ((4 * side_index + target_col % 4) // (2 * zc_count)).astype(jnp.float32)
    freq_z = jnp.arange(half_count, dtype=jnp.int32).astype(jnp.float32)
    p_first = (-256.0 + box_width * (freq_x[None, :] + 0.5 + node_first[:, None])).reshape(64, 1, 2, 1, 1, 1, 1)
    p_second = (-256.0 + box_width * (freq_y[None, :] + 0.5 + node_second[:, None])).reshape(64, 1, 1, 2, 1, 1, 1)
    p_third = (-256.0 + box_width * (freq_z[None, :] + 0.5 + node_third[:, None])).reshape(64, 1, 1, 1, 1, 1, half_count)
    angles = phase_angle(first, second, third, p_first, p_second, p_third)
    cosines = jnp.cos(angles)
    sine_part = jnp.sin(angles)
    result = jnp.stack([summed[0] * cosines + summed[1] * sine_part, summed[1] * cosines - summed[0] * sine_part])
    return result.reshape(2, 64, spatial, 2, 2, 16)

def advance(blocks, level_index):

    def one_device(device_index):
        dev_row = logical_index(device_index // N_BY, N_BX)
        dev_col = logical_index(device_index % N_BY, N_BY)
        mate_row = partner(dev_row, level_index)
        mate_col = partner(dev_col, level_index)
        summed = jnp.zeros((2, 64, SPAT_DEV, 2, 2, 2 ** level_index, 2, 8 // 2 ** level_index), jnp.float32)
        for source_row, source_col in ((dev_row, dev_col), (mate_row, dev_col), (dev_row, mate_col), (mate_row, mate_col)):
            source_block = blocks[physical_index(source_row, N_BX) * N_BY + physical_index(source_col, N_BY)]
            summed = summed + contribute(source_block, source_row, source_col, dev_row, dev_col, level_index, N_BY)
        return finish(summed, dev_row, dev_col, level_index, N_BY)
    return lax.map(one_device, jnp.arange(N_BX * N_BY, dtype=jnp.int32))

def reference(coefficients):
    blocks = coefficients.reshape(N_BX * N_BY, 2, 64, SPAT_DEV, 2, 2, 16)
    for level_index in range(2):
        blocks = advance(blocks, level_index)
    return blocks.reshape(N_BX, N_BY, 2, 64, PAIRS_DEV)
```

```python
import functools

import jax
import jax.numpy as jnp
import ml_dtypes
import numpy as np
from jax import lax
from jax.experimental import pallas as pl
from jax.experimental.pallas import tpu as pltpu
from jax.sharding import PartitionSpec as P

MESH = pl.DeviceIdType.MESH
NODES = [float(0.5 * np.cos((2 * k + 1) * np.pi / 8)) for k in range(4)]
SIN = [
    6.283182818516952,
    -41.341421395485554,
    81.59618379063296,
    -76.58009967534186,
    41.205391074799934,
    -12.271256275754906,
]
COS = [
    0.9999999891721036,
    -19.73920453203502,
    64.93911898074299,
    -85.45016549020424,
    60.16783121892548,
    -25.968311307335807,
    6.529607525848247,
]


def child_weights(bit):
    nodes = 0.5 * np.cos((2 * np.arange(4) + 1) * np.pi / 8)
    at = (bit - 0.5) / 2 + nodes / 2
    out = np.ones((4, 4))
    for t in range(4):
        for k in range(4):
            if k != t:
                out[t] *= (at - nodes[k]) / (nodes[t] - nodes[k])
    return out


def weights():
    side = [child_weights(0), child_weights(1)]
    blocks = [
        np.kron(np.kron(side[a], side[b]), side[c]) for a in (0, 1) for b in (0, 1) for c in (0, 1)
    ]
    whole = np.concatenate(blocks, axis=1)
    high = whole.astype(ml_dtypes.bfloat16)
    low = (whole - high.astype(np.float64)).astype(ml_dtypes.bfloat16)
    return np.concatenate([high, low], axis=0)


def sincos(turns):
    turns = turns - jnp.round(turns)
    square = turns * turns
    sine = jnp.full_like(turns, SIN[-1])
    for c in SIN[-2::-1]:
        sine = sine * square + c
    cosine = jnp.full_like(turns, COS[-1])
    for c in COS[-2::-1]:
        cosine = cosine * square + c
    return cosine, sine * turns


def kernel(
    x_ref, w_ref, o_ref, xin, xe, tab0, tab1, tab2, v, wh, wl, ob, mm, lin0, lin1, kap0, dkap,
    kap2, lin2, send1, recv1, send2, recv2, own,
):
    bx, by = lax.axis_index("bx"), lax.axis_index("by")
    a, b = bx // 4, by // 4
    row, col = lax.rem(bx, 4), lax.rem(by, 4)
    a0, a1, b0, b1 = a // 2, lax.rem(a, 2), b // 2, lax.rem(b, 2)
    me = 4 * a + b

    def flipped(k):
        p0 = lax.rem(a0 + k // 8, 2)
        q0 = lax.rem(b0 + k // 4 % 2, 2)
        p1 = lax.rem(a1 + k // 2 % 2, 2)
        q1 = lax.rem(b1 + k % 2, 2)
        return p0, q0, p1, q1

    def device(k):
        p0, q0, p1, q1 = flipped(k)
        return ((2 * p0 + p1) * 4 + row, (2 * q0 + q1) * 4 + col)

    def member(k):
        p0, q0, p1, q1 = flipped(k)
        return (2 * p0 + p1) * 4 + 2 * q0 + q1

    def lanes(m):
        return pl.ds(pl.multiple_of(m * 128, 128), 128)

    def inward(k):
        return pltpu.make_async_remote_copy(
            src_ref=x_ref.at[:, :, lanes(member(k))],
            dst_ref=xin.at[me],
            send_sem=send1.at[k],
            recv_sem=recv1.at[k],
            device_id=device(k),
            device_id_type=MESH,
        )

    def outward(k):
        return pltpu.make_async_remote_copy(
            src_ref=ob.at[k],
            dst_ref=o_ref.at[:, :, lanes(me)],
            send_sem=send2.at[k],
            recv_sem=recv2.at[k],
            device_id=device(k),
            device_id_type=MESH,
        )

    barrier = pltpu.get_barrier_semaphore()
    for k in range(1, 16):
        pl.semaphore_signal(barrier, inc=1, device_id=device(k), device_id_type=MESH)
    pl.semaphore_wait(barrier, 15)
    for k in (4, 12, 5, 13, 6, 14, 7, 15, 1, 9, 3, 11, 8, 2, 10):
        inward(k).start()
    own_in = pltpu.make_async_copy(x_ref.at[:, :, lanes(me)], xin.at[me], own.at[0])
    own_in.start()
    load_weights = pltpu.make_async_copy(w_ref, mm, own.at[1])
    load_weights.start()

    group = row * 4 + col
    px, py = group // 2, lax.rem(group, 2) * 4 + a
    lane = lax.broadcasted_iota(jnp.int32, (64, 128), 1)
    point = lax.broadcasted_iota(jnp.int32, (64, 128), 0)

    def node(digit):
        out = jnp.full((64, 128), NODES[3], jnp.float32)
        for k in range(3):
            out = jnp.where(digit == k, NODES[k], out)
        return out

    zx, zy, zz = node(point // 16), node(point // 4 % 4), node(point % 4)

    def lane_bit(index, width):
        return (index // width) % 2

    def as_f32(value):
        return value.astype(jnp.float32)

    ex, ey = as_f32(lane_bit(lane, 32)), as_f32(lane_bit(lane, 16))
    u8, u4 = lane_bit(lane, 8), lane_bit(lane, 4)
    u2, u1 = lane_bit(lane, 2), lane_bit(lane, 1)
    pz = 2 * b + lane_bit(lane, 64)
    cell_z0 = 2 * pz + u8
    cell_z1 = 2 * cell_z0 + u4
    small = (8, 128)

    def spread(value):
        return jnp.full(small, value, jnp.int32).astype(jnp.float32)

    def speed(sine_x, sine_y, cosine_z):
        return 0.05 * (1.0 + 0.5 * sine_x * sine_y + 0.3 * cosine_z)

    cos_z0 = sincos(as_f32(2 * cell_z0[0:8] + 1) * (1.0 / 32))[0]
    cos_z1 = sincos(as_f32(2 * cell_z1[0:8] + 1) * (1.0 / 64))[0]
    odd_z0, odd_z1 = as_f32(2 * cell_z0 + 1), as_f32(2 * cell_z1 + 1)

    def prepare0(c, _):
        odd_x, odd_y = 2 * (2 * px + c // 2) + 1, 2 * (2 * py + lax.rem(c, 2)) + 1
        sine_x = sincos(spread(odd_x) * (1.0 / 32))[1]
        sine_y = sincos(spread(odd_y) * (1.0 / 32))[1]
        kap0[c] = speed(sine_x, sine_y, cos_z0)
        wide_x, wide_y = odd_x.astype(jnp.float32), odd_y.astype(jnp.float32)
        lin0[c] = 0.5 + wide_x * zx + wide_y * zy + odd_z0 * zz
        sign_x = (2 * (c // 2) - 1).astype(jnp.float32)
        sign_y = (2 * lax.rem(c, 2) - 1).astype(jnp.float32)
        lin1[c] = 0.5 + sign_x * zx + sign_y * zy + as_f32(2 * u4 - 1) * zz
        return 0

    lax.fori_loop(0, 4, prepare0, 0)

    def prepare1(c, _):
        first, second = c // 4, lax.rem(c, 4)
        odd_x = 2 * (2 * (2 * px + first // 2) + second // 2) + 1
        odd_y = 2 * (2 * (2 * py + lax.rem(first, 2)) + lax.rem(second, 2)) + 1
        sine_x = sincos(spread(odd_x) * (1.0 / 64))[1]
        sine_y = sincos(spread(odd_y) * (1.0 / 64))[1]
        own_speed = speed(sine_x, sine_y, cos_z1)
        kap2[c] = own_speed
        dkap[c] = own_speed - kap0[first]
        wide_x, wide_y = odd_x.astype(jnp.float32), odd_y.astype(jnp.float32)
        lin2[c] = 2.0 * (wide_x * zx + wide_y * zy + odd_z1 * zz)
        return 0

    lax.fori_loop(0, 16, prepare1, 0)

    def radius(width, fx, fy, fz):
        p1 = width * (fx + zx) + (0.5 * width - 256.0)
        p2 = width * (fy + zy) + (0.5 * width - 256.0)
        p3 = width * (fz + zz) + (0.5 * width - 256.0)
        return jnp.sqrt(p1 * p1 + p2 * p2 + p3 * p3)

    def tall(value):
        return jnp.broadcast_to(value[None], (8, 8, 128)).reshape(64, 128)

    def fill0(n, _):
        fx = 4.0 * ex + (2 * (n // 16) + n // 4 % 2).astype(jnp.float32)
        fy = 4.0 * ey + (2 * (n // 8 % 2) + n // 2 % 2).astype(jnp.float32)
        fz = as_f32(8 * u2 + 4 * u1 + 2 * u4) + (n % 2).astype(jnp.float32)
        r = radius(32.0, fx, fy, fz)
        for c in range(4):
            cosine, sine = sincos(lin0[c] + tall(kap0[c]) * r)
            tab0[c * 32 + n, 0] = cosine
            tab0[c * 32 + n, 1] = sine
        return 0

    lax.fori_loop(0, 32, fill0, 0)

    def fill1(n, _):
        fx = 2.0 * ex + (n // 4).astype(jnp.float32)
        fy = 2.0 * ey + (n // 2 % 2).astype(jnp.float32)
        fz = as_f32(4 * u2 + 2 * u1) + (n % 2).astype(jnp.float32)
        r = radius(64.0, fx, fy, fz)

        def child(first, _):
            for second in range(4):
                c = first * 4 + second
                cosine, sine = sincos(lin1[second] + tall(dkap[c]) * r)
                tab1[c * 8 + n, 0] = cosine
                tab1[c * 8 + n, 1] = sine
            return 0

        lax.fori_loop(0, 4, child, 0)
        return 0

    lax.fori_loop(0, 8, fill1, 0)

    def fill2(c, _):
        r = radius(128.0, ex, ey, as_f32(2 * u2 + u1))
        cosine, sine = sincos(lin2[c] + tall(kap2[c]) * r)
        tab2[c, 0] = cosine
        tab2[c, 1] = sine
        return 0

    lax.fori_loop(0, 16, fill2, 0)

    even = (lane // 16) * 16 + 8 * u2 + 4 * u1 + 2 * u4

    def picked(value, index):
        return jnp.take_along_axis(value, index, axis=1, mode="promise_in_bounds")

    def arrange(k):
        p0, q0, p1, q1 = flipped(k)
        m = (2 * p0 + p1) * 4 + 2 * q0 + q1
        n = (2 * p1 + q1) * 8 + (2 * p0 + q0) * 2
        for part in range(2):
            got = xin[m, part]
            xe[n, part] = picked(got, even)
            xe[n + 1, part] = picked(got, even + 1)

    def arrive(k, _):
        inward(k).wait_recv()
        arrange(k)
        return 0

    load_weights.wait()
    own_in.wait()
    arrange(0)
    lax.fori_loop(1, 16, arrive, 0)

    def turn_and_sum(turns, data):
        for n in range(8):
            cosine, sine = turns(n)
            real, imag = data(n)
            out = (real * cosine - imag * sine, real * sine + imag * cosine)
            for part in range(2):
                high = out[part].astype(jnp.bfloat16)
                at = (pl.ds(64 * n, 64), pl.ds(128 * part, 128))
                wh[at] = high
                wl[at] = (out[part] - high.astype(jnp.float32)).astype(jnp.bfloat16)
        both = jnp.dot(mm[...], wh[...], preferred_element_type=jnp.float32)
        rest = jnp.dot(mm[0:64, :], wl[...], preferred_element_type=jnp.float32)
        total = both[0:64] + (both[64:128] + rest)
        return total[:, 0:128], total[:, 128:256]

    low4 = lane - 4 * u4

    def first_child(step, _):
        k0 = 3 - step
        c0 = 2 * lax.rem(a0 + k0 // 2, 2) + lax.rem(b0 + k0 % 2, 2)

        def first_level(g, _):
            sums = turn_and_sum(
                lambda n: (tab0[c0 * 32 + g * 8 + n, 0], tab0[c0 * 32 + g * 8 + n, 1]),
                lambda n: (xe[g * 8 + n, 0], xe[g * 8 + n, 1]),
            )
            for part in range(2):
                v[2 * g, part] = picked(sums[part], low4)
                v[2 * g + 1, part] = picked(sums[part], low4 + 4)
            return 0

        lax.fori_loop(0, 4, first_level, 0)

        def second_level(step1, _):
            k1 = 3 - step1
            c1 = 2 * lax.rem(a1 + k1 // 2, 2) + lax.rem(b1 + k1 % 2, 2)
            k, c = 4 * k0 + k1, 4 * c0 + c1
            real, imag = turn_and_sum(
                lambda n: (tab1[c * 8 + n, 0], tab1[c * 8 + n, 1]),
                lambda n: (v[n, 0], v[n, 1]),
            )
            cosine, sine = tab2[c, 0], tab2[c, 1]
            ob[k, 0] = real * cosine + imag * sine
            ob[k, 1] = imag * cosine - real * sine

            @pl.when(k > 0)
            def _():
                outward(k).start()

            return 0

        lax.fori_loop(0, 4, second_level, 0)
        return 0

    lax.fori_loop(0, 4, first_child, 0)

    own_out = pltpu.make_async_copy(ob.at[0], o_ref.at[:, :, lanes(me)], own.at[2])
    own_out.start()

    def finish(k, _):
        inward(k).wait_send()
        outward(k).wait_send()
        outward(k).wait_recv()
        return 0

    lax.fori_loop(1, 16, finish, 0)
    own_out.wait()


def local(coefficients):
    shape = coefficients.shape
    block = coefficients.reshape(shape[2:])
    f32, bf16 = jnp.float32, jnp.bfloat16
    out = pl.pallas_call(
        kernel,
        out_shape=jax.ShapeDtypeStruct(block.shape, f32),
        in_specs=[pl.BlockSpec(memory_space=pl.ANY)] * 2,
        out_specs=pl.BlockSpec(memory_space=pl.ANY),
        scratch_shapes=[
            pltpu.VMEM((16, 2, 64, 128), f32),
            pltpu.VMEM((32, 2, 64, 128), f32),
            pltpu.VMEM((128, 2, 64, 128), f32),
            pltpu.VMEM((128, 2, 64, 128), f32),
            pltpu.VMEM((16, 2, 64, 128), f32),
            pltpu.VMEM((8, 2, 64, 128), f32),
            pltpu.VMEM((512, 256), bf16),
            pltpu.VMEM((512, 256), bf16),
            pltpu.VMEM((16, 2, 64, 128), f32),
            pltpu.VMEM((128, 512), bf16),
            pltpu.VMEM((4, 64, 128), f32),
            pltpu.VMEM((4, 64, 128), f32),
            pltpu.VMEM((4, 8, 128), f32),
            pltpu.VMEM((16, 8, 128), f32),
            pltpu.VMEM((16, 8, 128), f32),
            pltpu.VMEM((16, 64, 128), f32),
            pltpu.SemaphoreType.DMA((16,)),
            pltpu.SemaphoreType.DMA((16,)),
            pltpu.SemaphoreType.DMA((16,)),
            pltpu.SemaphoreType.DMA((16,)),
            pltpu.SemaphoreType.DMA((3,)),
        ],
        compiler_params=pltpu.CompilerParams(
            collective_id=0, has_side_effects=True, vmem_limit_bytes=56 * 2**20
        ),
    )(block, jnp.asarray(weights()))
    return out.reshape(shape)


def solution(mesh):
    return jax.shard_map(
        local,
        mesh=mesh,
        in_specs=(P("bx", "by", None, None, None),),
        out_specs=P("bx", "by", None, None, None),
        check_vma=False,
    )
```

```python
import math

import jax
import jax.numpy as jnp
import numpy as np
from jax import lax
from jax.experimental import pallas as pl
from jax.experimental.pallas import tpu as pltpu
from jax.sharding import PartitionSpec as P

MESH = pl.DeviceIdType.MESH
NODES = [float(0.5 * np.cos((2 * k + 1) * np.pi / 8)) for k in range(4)]
SIN = [
    6.283182818516952,
    -41.341421395485554,
    81.59618379063296,
    -76.58009967534186,
    41.205391074799934,
    -12.271256275754906,
]
COS = [
    0.9999992215592304,
    -19.738982513358035,
    64.92872650603236,
    -85.27239557297074,
    58.79403136989473,
    -21.076769129657027,
]


def weights():
    row = lax.broadcasted_iota(jnp.int32, (64, 512), 0)
    column = lax.broadcasted_iota(jnp.int32, (64, 512), 1)

    def side(bit, t, s):
        at = 0.5 * (bit.astype(jnp.float32) - 0.5) + 0.5 * chosen(s, NODES)
        out = chosen(
            t, [1.0 / math.prod(NODES[t] - z for z in NODES if z != NODES[t]) for t in range(4)]
        )
        for k in range(4):
            out = jnp.where(t == k, out, out * (at - NODES[k]))
        return out

    first = side(column // 256, row // 16, column // 16 % 4)
    second = side(column // 128 % 2, row // 4 % 4, column // 4 % 4)
    return first * second * side(column // 64 % 2, row % 4, column % 4)


def chosen(digit, values):
    out = jnp.full(digit.shape, values[3], jnp.float32)
    for k in range(3):
        out = jnp.where(digit == k, values[k], out)
    return out


def sincos(turns):
    turns = turns - jnp.round(turns)
    square = turns * turns
    sine = jnp.full_like(turns, SIN[-1])
    for c in SIN[-2::-1]:
        sine = sine * square + c
    cosine = jnp.full_like(turns, COS[-1])
    for c in COS[-2::-1]:
        cosine = cosine * square + c
    return cosine, sine * turns


def kernel(
    x_ref, o_ref, xv, xp, xin, xe, r0, r1, squares, tab0, tab1, tab2, v, wh, wl, ob, mm, lin0, lin1,
    kap0, dkap, kap2, lin2, send1, recv1, send2, recv2, loads, own,
):
    bx, by = lax.axis_index("bx"), lax.axis_index("by")
    a, b = bx // 4, by // 4
    row, col = lax.rem(bx, 4), lax.rem(by, 4)
    a0, a1, b0, b1 = a // 2, lax.rem(a, 2), b // 2, lax.rem(b, 2)
    me = 4 * a + b

    def flipped(k):
        p0 = lax.rem(a0 + k // 8, 2)
        q0 = lax.rem(b0 + k // 4 % 2, 2)
        p1 = lax.rem(a1 + k // 2 % 2, 2)
        q1 = lax.rem(b1 + k % 2, 2)
        return p0, q0, p1, q1

    def device(k):
        p0, q0, p1, q1 = flipped(k)
        return ((2 * p0 + p1) * 4 + row, (2 * q0 + q1) * 4 + col)

    def member(k):
        p0, q0, p1, q1 = flipped(k)
        return (2 * p0 + p1) * 4 + 2 * q0 + q1

    def load(k):
        at = pl.ds(pl.multiple_of(member(k) * 128, 128), 128)
        return pltpu.make_async_copy(x_ref.at[:, :, at], xv.at[k], loads.at[k])

    def inward(half, k):
        return pltpu.make_async_remote_copy(
            src_ref=xp.at[half, k],
            dst_ref=xin.at[half, k],
            send_sem=send1.at[half, k],
            recv_sem=recv1.at[half, k],
            device_id=device(k),
            device_id_type=MESH,
        )

    def outward(half, k):
        return pltpu.make_async_remote_copy(
            src_ref=ob.at[half, k],
            dst_ref=o_ref.at[me, half],
            send_sem=send2.at[half, k],
            recv_sem=recv2.at[half, k],
            device_id=device(k),
            device_id_type=MESH,
        )

    order = (4, 12, 5, 13, 6, 14, 7, 15, 1, 9, 3, 11, 8, 2, 10)
    for k in order + (0,):
        load(k).start()
    barrier = pltpu.get_barrier_semaphore()
    for k in order:
        pl.semaphore_signal(barrier, inc=1, device_id=device(k), device_id_type=MESH)
    lane = lax.broadcasted_iota(jnp.int32, (64, 128), 1)
    point = lax.broadcasted_iota(jnp.int32, (64, 128), 0)
    first_part = lane < 64

    def swapped(value):
        return pltpu.roll(value, 64, axis=1)

    def pack(k, into):
        real, imag = xv[k, 0], xv[k, 1]
        into[0, k] = jnp.where(first_part, real, swapped(imag))
        into[1, k] = jnp.where(first_part, swapped(real), imag)

    for k in order:
        load(k).wait()
        pack(k, xp)
    pl.semaphore_wait(barrier, 15)
    for half in range(2):
        for k in order:
            inward(half, k).start()
    load(0).wait()
    pack(0, xin)

    group = row * 4 + col
    px, py = group // 2, lax.rem(group, 2) * 4 + a
    zx, zy, zz = (chosen(point // w % 4, NODES) for w in (16, 4, 1))

    def lane_bit(index, width):
        return (index // width) % 2

    def as_f32(value):
        return value.astype(jnp.float32)

    ex, ey = as_f32(lane_bit(lane, 32)), as_f32(lane_bit(lane, 16))
    child, u8, u4 = lane_bit(lane, 64), lane_bit(lane, 8), lane_bit(lane, 4)
    u2, u1 = lane_bit(lane, 2), lane_bit(lane, 1)
    whole = weights()
    leading = whole.astype(jnp.bfloat16)
    mm[0:64, :] = leading
    mm[64:128, :] = (whole - leading.astype(jnp.float32)).astype(jnp.bfloat16)

    def speed(odd_x, odd_y, odd_z, scale):
        sine_x = sincos(as_f32(odd_x[0:8]) * scale)[1]
        sine_y = sincos(as_f32(odd_y[0:8]) * scale)[1]
        cosine_z = sincos(as_f32(odd_z[0:8]) * scale)[0]
        return 0.05 * (1.0 + 0.5 * sine_x * sine_y + 0.3 * cosine_z)

    def full(value):
        return jnp.full((64, 128), value, jnp.int32)

    def linear(odd_x, odd_y, odd_z):
        return as_f32(odd_x) * zx + as_f32(odd_y) * zy + as_f32(odd_z) * zz

    def prepare0(c, _):
        odd_x = 2 * (2 * px + child) + 1
        odd_y = full(2 * (2 * py + lax.rem(c, 2)) + 1)
        odd_z = 2 * (2 * (2 * b + c // 2) + u8) + 1
        kap0[c] = speed(odd_x, odd_y, odd_z, 1.0 / 32)
        lin0[c] = 0.5 + linear(odd_x, odd_y, odd_z)
        return 0

    lax.fori_loop(0, 4, prepare0, 0)

    def prepare1(c, _):
        cell_x, cell_y = 2 * px + c // 4 % 2, 2 * py + c // 2 % 2
        cell_z = 2 * (2 * b + c // 8) + u8
        parent = speed(full(2 * cell_x + 1), full(2 * cell_y + 1), 2 * cell_z + 1, 1.0 / 32)
        odd_x = full(2 * (2 * cell_x + lax.rem(c, 2)) + 1)
        odd_y, odd_z = 2 * (2 * cell_y + child) + 1, 2 * (2 * cell_z + u4) + 1
        kap2[c] = speed(odd_x, odd_y, odd_z, 1.0 / 64)
        dkap[c] = kap2[c] - parent
        lin2[c] = 2.0 * linear(odd_x, odd_y, odd_z)
        return 0

    lax.fori_loop(0, 16, prepare1, 0)
    for c in range(2):
        lin1[c] = 0.5 + linear(full(2 * c - 1), 2 * child - 1, 2 * u4 - 1)

    def square(width, at):
        p = width * at + (0.5 * width - 256.0)
        return p * p

    for n in range(4):
        squares[n] = square(32.0, 4.0 * ex + n + zx)
        squares[4 + n] = square(32.0, 4.0 * ey + n + zy)
    for n in range(2):
        squares[8 + n] = square(32.0, as_f32(8 * u2 + 4 * u1 + 2 * u4 + n) + zz)
        squares[10 + n] = square(64.0, 2.0 * ex + n + zx)
        squares[12 + n] = square(64.0, 2.0 * ey + n + zy)
        squares[14 + n] = square(64.0, as_f32(4 * u2 + 2 * u1 + n) + zz)

    def radius0(n, _):
        fx, fy = 2 * (n // 16) + n // 4 % 2, 2 * (n // 8 % 2) + n // 2 % 2
        r0[n] = jnp.sqrt(squares[fx] + squares[4 + fy] + squares[8 + n % 2])
        return 0

    def radius1(n, _):
        r1[n] = jnp.sqrt(squares[10 + n // 4] + squares[12 + n // 2 % 2] + squares[14 + n % 2])
        return 0

    lax.fori_loop(0, 32, radius0, 0)
    lax.fori_loop(0, 8, radius1, 0)
    r1[8] = jnp.sqrt(
        square(128.0, ex + zx) + square(128.0, ey + zy) + square(128.0, as_f32(2 * u2 + u1) + zz)
    )

    def tall(value):
        return jnp.broadcast_to(value[None], (8, 8, 128)).reshape(64, 128)

    def keep(table, at, turns):
        table[at, 0], table[at, 1] = sincos(turns)

    def fill(half):
        def fill0(n, _):
            for cy in range(2):
                c = half * 2 + cy
                keep(tab0, c * 32 + n, lin0[c] + tall(kap0[c]) * r0[n])
            return 0

        def fill1(step, _):
            first, n = step // 8, step % 8
            for dx in range(2):
                c = half * 8 + first * 2 + dx
                keep(tab1, c * 8 + n, lin1[dx] + tall(dkap[c]) * r1[n])
            return 0

        def fill2(step, _):
            c = half * 8 + step
            keep(tab2, c, lin2[c] + tall(kap2[c]) * r1[8])
            return 0

        lax.fori_loop(0, 32, fill0, 0)
        lax.fori_loop(0, 32, fill1, 0)
        lax.fori_loop(0, 8, fill2, 0)

    even = (lane // 16) % 4 * 16 + 8 * u2 + 4 * u1 + 2 * u4
    low4 = lane % 64 - 4 * u4

    def picked(value, index):
        return jnp.take_along_axis(value, index, axis=1, mode="promise_in_bounds")

    def arrange(half, k):
        p0, q0, p1, q1 = flipped(k)
        n = (2 * p1 + q1) * 8 + (2 * p0 + q0) * 2
        got = xin[half, k]
        for bit in range(2):
            for part in range(2):
                xe[n + bit, part] = picked(got, even + (bit + 64 * part))

    def turn_and_sum(data, table, at):
        for n in range(8):
            real, imag = data(n)
            cosine, sine = table[at + n, 0], table[at + n, 1]
            out = (real * cosine - imag * sine, real * sine + imag * cosine)
            for part in range(2):
                high = out[part].astype(jnp.bfloat16)
                where = (pl.ds(64 * n, 64), pl.ds(128 * part, 128))
                wh[where] = high
                wl[where] = (out[part] - high.astype(jnp.float32)).astype(jnp.bfloat16)
        both = jnp.dot(mm[...], wh[...], preferred_element_type=jnp.float32)
        rest = jnp.dot(mm[0:64, :], wl[...], preferred_element_type=jnp.float32)
        total = both[0:64] + (both[64:128] + rest)
        return total[:, 0:128], total[:, 128:256]

    def box(half, _):
        arrange(half, 0)

        def arrive(k, _):
            inward(half, k).wait_recv()
            arrange(half, k)
            return 0

        lax.fori_loop(1, 16, arrive, 0)

        def first_y(step, _):
            cy = lax.rem(b0 + 1 - step, 2)

            def first_level(g, _):
                sums = turn_and_sum(
                    lambda n: (xe[g * 8 + n, 0], xe[g * 8 + n, 1]),
                    tab0,
                    (half * 2 + cy) * 32 + g * 8,
                )
                for cx in range(2):
                    for bit in range(2):
                        for part in range(2):
                            v[cx * 8 + 2 * g + bit, part] = picked(
                                sums[part], low4 + (64 * cx + 4 * bit)
                            )
                return 0

            lax.fori_loop(0, 4, first_level, 0)

            def second_level(last, _):
                fx0, fx1 = 1 - last // 2, 1 - lax.rem(last, 2)
                cx, dx = lax.rem(a0 + fx0, 2), lax.rem(a1 + fx1, 2)
                c = half * 8 + cx * 4 + cy * 2 + dx
                real, imag = turn_and_sum(lambda n: (v[cx * 8 + n, 0], v[cx * 8 + n, 1]), tab1, c * 8)
                cosine, sine = tab2[c, 0], tab2[c, 1]
                into = (real * cosine + imag * sine, imag * cosine - real * sine)
                for dy in range(2):
                    k = 8 * fx0 + 4 * (1 - step) + 2 * fx1 + lax.rem(b1 + dy, 2)
                    if dy == 0:
                        ob[half, k] = jnp.where(first_part, into[0], swapped(into[1]))
                    else:
                        ob[half, k] = jnp.where(first_part, swapped(into[0]), into[1])

                    @pl.when(k > 0)
                    def _():
                        outward(half, k).start()

                return 0

            lax.fori_loop(0, 4, second_level, 0)
            return 0

        lax.fori_loop(0, 2, first_y, 0)
        return 0

    fill(0)
    fill(1)
    lax.fori_loop(0, 2, box, 0)
    own_out = [pltpu.make_async_copy(ob.at[h, 0], o_ref.at[me, h], own.at[h]) for h in range(2)]
    for copy in own_out:
        copy.start()

    def finish(k, _):
        for half in range(2):
            inward(half, k).wait_send()
            outward(half, k).wait_send()
            outward(half, k).wait_recv()
        return 0

    lax.fori_loop(1, 16, finish, 0)
    for copy in own_out:
        copy.wait()


def unpack(p_ref, o_ref, buf, sems):
    first_part = lax.broadcasted_iota(jnp.int32, (64, 128), 1) < 64
    copies = []
    for m in range(16):
        one, two = p_ref[m, 0], p_ref[m, 1]
        buf[m, 0] = jnp.where(first_part, one, pltpu.roll(two, 64, axis=1))
        buf[m, 1] = jnp.where(first_part, pltpu.roll(one, 64, axis=1), two)
        copy = pltpu.make_async_copy(buf.at[m], o_ref.at[:, :, pl.ds(128 * m, 128)], sems.at[m])
        copy.start()
        copies.append(copy)
    for copy in copies:
        copy.wait()


def local(coefficients):
    shape = coefficients.shape
    block = coefficients.reshape(shape[2:])
    f32, bf16 = jnp.float32, jnp.bfloat16
    packed = pl.pallas_call(
        kernel,
        out_shape=jax.ShapeDtypeStruct((16, 2, 64, 128), f32),
        in_specs=[pl.BlockSpec(memory_space=pl.ANY)],
        out_specs=pl.BlockSpec(memory_space=pl.ANY),
        scratch_shapes=[
            pltpu.VMEM((16, 2, 64, 128), f32),
            pltpu.VMEM((2, 16, 64, 128), f32),
            pltpu.VMEM((2, 16, 64, 128), f32),
            pltpu.VMEM((32, 2, 64, 128), f32),
            pltpu.VMEM((32, 64, 128), f32),
            pltpu.VMEM((9, 64, 128), f32),
            pltpu.VMEM((16, 64, 128), f32),
            pltpu.VMEM((128, 2, 64, 128), f32),
            pltpu.VMEM((128, 2, 64, 128), f32),
            pltpu.VMEM((16, 2, 64, 128), f32),
            pltpu.VMEM((16, 2, 64, 128), f32),
            pltpu.VMEM((512, 256), bf16),
            pltpu.VMEM((512, 256), bf16),
            pltpu.VMEM((2, 16, 64, 128), f32),
            pltpu.VMEM((128, 512), bf16),
            pltpu.VMEM((4, 64, 128), f32),
            pltpu.VMEM((2, 64, 128), f32),
            pltpu.VMEM((4, 8, 128), f32),
            pltpu.VMEM((16, 8, 128), f32),
            pltpu.VMEM((16, 8, 128), f32),
            pltpu.VMEM((16, 64, 128), f32),
            pltpu.SemaphoreType.DMA((2, 16)),
            pltpu.SemaphoreType.DMA((2, 16)),
            pltpu.SemaphoreType.DMA((2, 16)),
            pltpu.SemaphoreType.DMA((2, 16)),
            pltpu.SemaphoreType.DMA((16,)),
            pltpu.SemaphoreType.DMA((2,)),
        ],
        compiler_params=pltpu.CompilerParams(
            collective_id=0, has_side_effects=True, vmem_limit_bytes=52 * 2**20
        ),
    )(block)
    out = pl.pallas_call(
        unpack,
        out_shape=jax.ShapeDtypeStruct(block.shape, f32),
        in_specs=[pl.BlockSpec(memory_space=pltpu.VMEM)],
        out_specs=pl.BlockSpec(memory_space=pl.ANY),
        scratch_shapes=[pltpu.VMEM((16, 2, 64, 128), f32), pltpu.SemaphoreType.DMA((16,))],
        compiler_params=pltpu.CompilerParams(vmem_limit_bytes=16 * 2**20),
    )(packed)
    return out.reshape(shape)


def solution(mesh):
    return jax.shard_map(
        local,
        mesh=mesh,
        in_specs=(P("bx", "by", None, None, None),),
        out_specs=P("bx", "by", None, None, None),
        check_vma=False,
    )
```

```python
import math

import jax
import jax.numpy as jnp
import numpy as np
from jax import lax
from jax.experimental import pallas as pl
from jax.experimental.pallas import tpu as pltpu
from jax.sharding import PartitionSpec as P

MESH = pl.DeviceIdType.MESH
NODES = [float(0.5 * np.cos((2 * k + 1) * np.pi / 8)) for k in range(4)]
SIN = [
    6.283182818516952,
    -41.341421395485554,
    81.59618379063296,
    -76.58009967534186,
    41.205391074799934,
    -12.271256275754906,
]
COS = [
    0.9999992215592304,
    -19.738982513358035,
    64.92872650603236,
    -85.27239557297074,
    58.79403136989473,
    -21.076769129657027,
]


def weights():
    row = lax.broadcasted_iota(jnp.int32, (64, 512), 0)
    column = lax.broadcasted_iota(jnp.int32, (64, 512), 1)

    def side(bit, t, s):
        at = 0.5 * (bit.astype(jnp.float32) - 0.5) + 0.5 * chosen(s, NODES)
        out = chosen(
            t, [1.0 / math.prod(NODES[t] - z for z in NODES if z != NODES[t]) for t in range(4)]
        )
        for k in range(4):
            out = jnp.where(t == k, out, out * (at - NODES[k]))
        return out

    first = side(column // 256, row // 16, column // 16 % 4)
    second = side(column // 128 % 2, row // 4 % 4, column // 4 % 4)
    return first * second * side(column // 64 % 2, row % 4, column % 4)


def chosen(digit, values):
    out = jnp.full(digit.shape, values[3], jnp.float32)
    for k in range(3):
        out = jnp.where(digit == k, values[k], out)
    return out


def sincos(turns):
    turns = turns - jnp.round(turns)
    square = turns * turns
    sine = jnp.full_like(turns, SIN[-1])
    for c in SIN[-2::-1]:
        sine = sine * square + c
    cosine = jnp.full_like(turns, COS[-1])
    for c in COS[-2::-1]:
        cosine = cosine * square + c
    return cosine, sine * turns


def kernel(
    x_ref, o_ref, xv, xp, xin, xe, r0, r1, squares, tab0, tab1, tab2, v, wh, wl, ob, mm, lin0, lin1,
    kap0, dkap, kap2, lin2, send1, recv1, send2, recv2, loads, own,
    told,
):
    bx, by = lax.axis_index("bx"), lax.axis_index("by")
    a, b = bx // 4, by // 4
    row, col = lax.rem(bx, 4), lax.rem(by, 4)
    a0, a1, b0, b1 = a // 2, lax.rem(a, 2), b // 2, lax.rem(b, 2)
    me = 4 * a + b

    def ahead(k):
        return lax.rem(a + k // 4, 4), lax.rem(b + k % 4, 4)

    def device(place):
        return (place[0] * 4 + row, place[1] * 4 + col)

    def flipped(k):
        x = 2 * lax.rem(a0 + k // 8, 2) + lax.rem(a1 + k // 4 % 2, 2)
        y = 2 * lax.rem(b0 + k // 2 % 2, 2) + lax.rem(b1 + k % 2, 2)
        return x, y

    def load(k):
        x, y = ahead(k)
        at = pl.ds(pl.multiple_of((4 * x + y) * 128, 128), 128)
        return pltpu.make_async_copy(x_ref.at[:, :, at], xv.at[k], loads.at[k])

    def inward(half, k):
        return pltpu.make_async_remote_copy(
            src_ref=xp.at[half, k],
            dst_ref=xin.at[half, k],
            send_sem=send1.at[half, k],
            recv_sem=recv1.at[half, k],
            device_id=device(ahead(k)),
            device_id_type=MESH,
        )

    def outward(half, k):
        return pltpu.make_async_remote_copy(
            src_ref=ob.at[half, k],
            dst_ref=o_ref.at[me, half],
            send_sem=send2.at[half, k],
            recv_sem=recv2.at[half, k],
            device_id=device(flipped(k)),
            device_id_type=MESH,
        )

    along_z, along_y = (1, 2, 3), (4, 8, 12)
    straight = along_z + along_y
    order = straight + (6, 10, 14, 5, 9, 13, 7, 11, 15)
    for k in order + (0,):
        load(k).start()
    barrier = pltpu.get_barrier_semaphore()
    for k in straight:
        pl.semaphore_signal(barrier, inc=1, device_id=device(ahead(k)), device_id_type=MESH)
    lane = lax.broadcasted_iota(jnp.int32, (64, 128), 1)
    point = lax.broadcasted_iota(jnp.int32, (64, 128), 0)
    first_part = lane < 64

    def swapped(value):
        return pltpu.roll(value, 64, axis=1)

    def pack(k, into):
        real, imag = xv[k, 0], xv[k, 1]
        into[0, k] = jnp.where(first_part, real, swapped(imag))
        into[1, k] = jnp.where(first_part, swapped(real), imag)

    for k in order:
        load(k).wait()
        pack(k, xp)
    pl.semaphore_wait(barrier, 6)
    for k in along_y:
        pl.semaphore_signal(told, inc=1, device_id=device(ahead(k)), device_id_type=MESH)
    for k in straight:
        inward(0, k).start()
    pl.semaphore_wait(told, 3)
    for k in order[6:]:
        inward(0, k).start()
    for k in straight:
        inward(1, k).start()
    for k in order[6:]:
        inward(1, k).start()
    load(0).wait()
    pack(0, xin)

    group = row * 4 + col
    px, py = group // 2, lax.rem(group, 2) * 4 + a
    zx, zy, zz = (chosen(point // w % 4, NODES) for w in (16, 4, 1))

    def lane_bit(index, width):
        return (index // width) % 2

    def as_f32(value):
        return value.astype(jnp.float32)

    ex, ey = as_f32(lane_bit(lane, 32)), as_f32(lane_bit(lane, 16))
    child, u8, u4 = lane_bit(lane, 64), lane_bit(lane, 8), lane_bit(lane, 4)
    u2, u1 = lane_bit(lane, 2), lane_bit(lane, 1)
    whole = weights()
    leading = whole.astype(jnp.bfloat16)
    mm[0:64, :] = leading
    mm[64:128, :] = (whole - leading.astype(jnp.float32)).astype(jnp.bfloat16)

    def speed(odd_x, odd_y, odd_z, scale):
        sine_x = sincos(as_f32(odd_x[0:8]) * scale)[1]
        sine_y = sincos(as_f32(odd_y[0:8]) * scale)[1]
        cosine_z = sincos(as_f32(odd_z[0:8]) * scale)[0]
        return 0.05 * (1.0 + 0.5 * sine_x * sine_y + 0.3 * cosine_z)

    def full(value):
        return jnp.full((64, 128), value, jnp.int32)

    def linear(odd_x, odd_y, odd_z):
        return as_f32(odd_x) * zx + as_f32(odd_y) * zy + as_f32(odd_z) * zz

    def prepare0(c, _):
        odd_x = 2 * (2 * px + child) + 1
        odd_y = full(2 * (2 * py + lax.rem(c, 2)) + 1)
        odd_z = 2 * (2 * (2 * b + c // 2) + u8) + 1
        kap0[c] = speed(odd_x, odd_y, odd_z, 1.0 / 32)
        lin0[c] = 0.5 + linear(odd_x, odd_y, odd_z)
        return 0

    lax.fori_loop(0, 4, prepare0, 0)

    def prepare1(c, _):
        cell_x, cell_y = 2 * px + c // 4 % 2, 2 * py + c // 2 % 2
        cell_z = 2 * (2 * b + c // 8) + u8
        parent = speed(full(2 * cell_x + 1), full(2 * cell_y + 1), 2 * cell_z + 1, 1.0 / 32)
        odd_x = full(2 * (2 * cell_x + lax.rem(c, 2)) + 1)
        odd_y, odd_z = 2 * (2 * cell_y + child) + 1, 2 * (2 * cell_z + u4) + 1
        kap2[c] = speed(odd_x, odd_y, odd_z, 1.0 / 64)
        dkap[c] = kap2[c] - parent
        lin2[c] = 2.0 * linear(odd_x, odd_y, odd_z)
        return 0

    lax.fori_loop(0, 16, prepare1, 0)
    for c in range(2):
        lin1[c] = 0.5 + linear(full(2 * c - 1), 2 * child - 1, 2 * u4 - 1)

    def square(width, at):
        p = width * at + (0.5 * width - 256.0)
        return p * p

    for n in range(4):
        squares[n] = square(32.0, 4.0 * ex + n + zx)
        squares[4 + n] = square(32.0, 4.0 * ey + n + zy)
    for n in range(2):
        squares[8 + n] = square(32.0, as_f32(8 * u2 + 4 * u1 + 2 * u4 + n) + zz)
        squares[10 + n] = square(64.0, 2.0 * ex + n + zx)
        squares[12 + n] = square(64.0, 2.0 * ey + n + zy)
        squares[14 + n] = square(64.0, as_f32(4 * u2 + 2 * u1 + n) + zz)

    def radius0(n, _):
        fx, fy = 2 * (n // 16) + n // 4 % 2, 2 * (n // 8 % 2) + n // 2 % 2
        r0[n] = jnp.sqrt(squares[fx] + squares[4 + fy] + squares[8 + n % 2])
        return 0

    def radius1(n, _):
        r1[n] = jnp.sqrt(squares[10 + n // 4] + squares[12 + n // 2 % 2] + squares[14 + n % 2])
        return 0

    lax.fori_loop(0, 32, radius0, 0)
    lax.fori_loop(0, 8, radius1, 0)
    r1[8] = jnp.sqrt(
        square(128.0, ex + zx) + square(128.0, ey + zy) + square(128.0, as_f32(2 * u2 + u1) + zz)
    )

    def tall(value):
        return jnp.broadcast_to(value[None], (8, 8, 128)).reshape(64, 128)

    def keep(table, at, turns):
        table[at, 0], table[at, 1] = sincos(turns)

    def fill(half):
        def fill0(n, _):
            for cy in range(2):
                c = half * 2 + cy
                keep(tab0, c * 32 + n, lin0[c] + tall(kap0[c]) * r0[n])
            return 0

        def fill1(step, _):
            first, n = step // 8, step % 8
            for dx in range(2):
                c = half * 8 + first * 2 + dx
                keep(tab1, c * 8 + n, lin1[dx] + tall(dkap[c]) * r1[n])
            return 0

        def fill2(step, _):
            c = half * 8 + step
            keep(tab2, c, lin2[c] + tall(kap2[c]) * r1[8])
            return 0

        lax.fori_loop(0, 32, fill0, 0)
        lax.fori_loop(0, 32, fill1, 0)
        lax.fori_loop(0, 8, fill2, 0)

    even = (lane // 16) % 4 * 16 + 8 * u2 + 4 * u1 + 2 * u4
    low4 = lane % 64 - 4 * u4

    def picked(value, index):
        return jnp.take_along_axis(value, index, axis=1, mode="promise_in_bounds")

    def arrange(half, k):
        x, y = lax.rem(a + 4 - k // 4, 4), lax.rem(b + 4 - k % 4, 4)
        n = (2 * (x % 2) + y % 2) * 8 + (2 * (x // 2) + y // 2) * 2
        got = xin[half, k]
        for bit in range(2):
            for part in range(2):
                xe[n + bit, part] = picked(got, even + (bit + 64 * part))

    def turn_and_sum(data, table, at):
        for n in range(8):
            real, imag = data(n)
            cosine, sine = table[at + n, 0], table[at + n, 1]
            out = (real * cosine - imag * sine, real * sine + imag * cosine)
            for part in range(2):
                high = out[part].astype(jnp.bfloat16)
                where = (pl.ds(64 * n, 64), pl.ds(128 * part, 128))
                wh[where] = high
                wl[where] = (out[part] - high.astype(jnp.float32)).astype(jnp.bfloat16)
        both = jnp.dot(mm[...], wh[...], preferred_element_type=jnp.float32)
        rest = jnp.dot(mm[0:64, :], wl[...], preferred_element_type=jnp.float32)
        total = both[0:64] + (both[64:128] + rest)
        return total[:, 0:128], total[:, 128:256]

    def box(half, _):
        arrange(half, 0)

        def arrive(k, _):
            inward(half, k).wait_recv()
            arrange(half, k)
            return 0

        lax.fori_loop(1, 16, arrive, 0)

        def first_level(step, _):
            cy, g = step // 4, step % 4
            sums = turn_and_sum(
                lambda n: (xe[g * 8 + n, 0], xe[g * 8 + n, 1]), tab0, (half * 2 + cy) * 32 + g * 8
            )
            for cx in range(2):
                for bit in range(2):
                    for part in range(2):
                        v[cx * 16 + cy * 8 + 2 * g + bit, part] = picked(
                            sums[part], low4 + (64 * cx + 4 * bit)
                        )
            return 0

        lax.fori_loop(0, 8, first_level, 0)

        def second_level(step, _):
            flips = (11 - step) % 8
            fx0, fx1, fy0 = flips // 2 % 2, flips // 1 % 2, flips // 4 % 2
            cx, dx, cy = lax.rem(a0 + fx0, 2), lax.rem(a1 + fx1, 2), lax.rem(b0 + fy0, 2)
            at, c = cx * 16 + cy * 8, half * 8 + cx * 4 + cy * 2 + dx
            real, imag = turn_and_sum(lambda n: (v[at + n, 0], v[at + n, 1]), tab1, c * 8)
            cosine, sine = tab2[c, 0], tab2[c, 1]
            into = (real * cosine + imag * sine, imag * cosine - real * sine)
            for dy in range(2):
                k = 8 * fx0 + 4 * fx1 + 2 * fy0 + lax.rem(b1 + dy, 2)
                if dy == 0:
                    ob[half, k] = jnp.where(first_part, into[0], swapped(into[1]))
                else:
                    ob[half, k] = jnp.where(first_part, swapped(into[0]), into[1])

                @pl.when(k > 0)
                def _():
                    outward(half, k).start()

            return 0

        lax.fori_loop(0, 8, second_level, 0)
        return 0

    fill(0)
    fill(1)
    lax.fori_loop(0, 2, box, 0)
    own_out = [pltpu.make_async_copy(ob.at[h, 0], o_ref.at[me, h], own.at[h]) for h in range(2)]
    for copy in own_out:
        copy.start()

    def finish(k, _):
        for half in range(2):
            inward(half, k).wait_send()
            outward(half, k).wait_send()
            outward(half, k).wait_recv()
        return 0

    lax.fori_loop(1, 16, finish, 0)
    for copy in own_out:
        copy.wait()


def unpack(p_ref, o_ref, buf, sems):
    first_part = lax.broadcasted_iota(jnp.int32, (64, 128), 1) < 64
    copies = []
    for m in range(16):
        one, two = p_ref[m, 0], p_ref[m, 1]
        buf[m, 0] = jnp.where(first_part, one, pltpu.roll(two, 64, axis=1))
        buf[m, 1] = jnp.where(first_part, pltpu.roll(one, 64, axis=1), two)
        copy = pltpu.make_async_copy(buf.at[m], o_ref.at[:, :, pl.ds(128 * m, 128)], sems.at[m])
        copy.start()
        copies.append(copy)
    for copy in copies:
        copy.wait()


def local(coefficients):
    shape = coefficients.shape
    block = coefficients.reshape(shape[2:])
    f32, bf16 = jnp.float32, jnp.bfloat16
    packed = pl.pallas_call(
        kernel,
        out_shape=jax.ShapeDtypeStruct((16, 2, 64, 128), f32),
        in_specs=[pl.BlockSpec(memory_space=pl.ANY)],
        out_specs=pl.BlockSpec(memory_space=pl.ANY),
        scratch_shapes=[
            pltpu.VMEM((16, 2, 64, 128), f32),
            pltpu.VMEM((2, 16, 64, 128), f32),
            pltpu.VMEM((2, 16, 64, 128), f32),
            pltpu.VMEM((32, 2, 64, 128), f32),
            pltpu.VMEM((32, 64, 128), f32),
            pltpu.VMEM((9, 64, 128), f32),
            pltpu.VMEM((16, 64, 128), f32),
            pltpu.VMEM((128, 2, 64, 128), f32),
            pltpu.VMEM((128, 2, 64, 128), f32),
            pltpu.VMEM((16, 2, 64, 128), f32),
            pltpu.VMEM((32, 2, 64, 128), f32),
            pltpu.VMEM((512, 256), bf16),
            pltpu.VMEM((512, 256), bf16),
            pltpu.VMEM((2, 16, 64, 128), f32),
            pltpu.VMEM((128, 512), bf16),
            pltpu.VMEM((4, 64, 128), f32),
            pltpu.VMEM((2, 64, 128), f32),
            pltpu.VMEM((4, 8, 128), f32),
            pltpu.VMEM((16, 8, 128), f32),
            pltpu.VMEM((16, 8, 128), f32),
            pltpu.VMEM((16, 64, 128), f32),
            pltpu.SemaphoreType.DMA((2, 16)),
            pltpu.SemaphoreType.DMA((2, 16)),
            pltpu.SemaphoreType.DMA((2, 16)),
            pltpu.SemaphoreType.DMA((2, 16)),
            pltpu.SemaphoreType.DMA((16,)),
            pltpu.SemaphoreType.DMA((2,)),
            pltpu.SemaphoreType.REGULAR,
        ],
        compiler_params=pltpu.CompilerParams(
            collective_id=0, has_side_effects=True, vmem_limit_bytes=52 * 2**20
        ),
    )(block)
    out = pl.pallas_call(
        unpack,
        out_shape=jax.ShapeDtypeStruct(block.shape, f32),
        in_specs=[pl.BlockSpec(memory_space=pltpu.VMEM)],
        out_specs=pl.BlockSpec(memory_space=pl.ANY),
        scratch_shapes=[pltpu.VMEM((16, 2, 64, 128), f32), pltpu.SemaphoreType.DMA((16,))],
        compiler_params=pltpu.CompilerParams(vmem_limit_bytes=16 * 2**20),
    )(packed)
    return out.reshape(shape)


def solution(mesh):
    return jax.shard_map(
        local,
        mesh=mesh,
        in_specs=(P("bx", "by", None, None, None),),
        out_specs=P("bx", "by", None, None, None),
        check_vma=False,
    )
```

```python
import math

import jax
import jax.numpy as jnp
import numpy as np
from jax import lax
from jax.experimental import pallas as pl
from jax.experimental.pallas import tpu as pltpu
from jax.sharding import PartitionSpec as P

MESH = pl.DeviceIdType.MESH
NODES = [float(0.5 * np.cos((2 * k + 1) * np.pi / 8)) for k in range(4)]
SIN = [
    6.283182818516952,
    -41.341421395485554,
    81.59618379063296,
    -76.58009967534186,
    41.205391074799934,
    -12.271256275754906,
]
COS = [
    0.9999992215592304,
    -19.738982513358035,
    64.92872650603236,
    -85.27239557297074,
    58.79403136989473,
    -21.076769129657027,
]


def weights():
    row = lax.broadcasted_iota(jnp.int32, (64, 512), 0)
    column = lax.broadcasted_iota(jnp.int32, (64, 512), 1)

    def side(bit, t, s):
        at = 0.5 * (bit.astype(jnp.float32) - 0.5) + 0.5 * chosen(s, NODES)
        out = chosen(
            t, [1.0 / math.prod(NODES[t] - z for z in NODES if z != NODES[t]) for t in range(4)]
        )
        for k in range(4):
            out = jnp.where(t == k, out, out * (at - NODES[k]))
        return out

    first = side(column // 256, row // 16, column // 16 % 4)
    second = side(column // 128 % 2, row // 4 % 4, column // 4 % 4)
    return first * second * side(column // 64 % 2, row % 4, column % 4)


def chosen(digit, values):
    out = jnp.full(digit.shape, values[3], jnp.float32)
    for k in range(3):
        out = jnp.where(digit == k, values[k], out)
    return out


def sincos(turns):
    turns = turns - jnp.round(turns)
    square = turns * turns
    sine = jnp.full_like(turns, SIN[-1])
    for c in SIN[-2::-1]:
        sine = sine * square + c
    cosine = jnp.full_like(turns, COS[-1])
    for c in COS[-2::-1]:
        cosine = cosine * square + c
    return cosine, sine * turns


def kernel(
    x_ref, o_ref, xv, xp, xin, xe, r0, r1, squares, tab0, tab1, tab2, v, wh, wl, ob, mm, lin0, lin1,
    kap0, dkap, kap2, lin2, send1, recv1, send2, recv2, loads, own,
    told,
):
    bx, by = lax.axis_index("bx"), lax.axis_index("by")
    a, b = bx // 4, by // 4
    row, col = lax.rem(bx, 4), lax.rem(by, 4)
    a0, a1, b0, b1 = a // 2, lax.rem(a, 2), b // 2, lax.rem(b, 2)
    me = 4 * a + b

    def ahead(k):
        return lax.rem(a + k // 4, 4), lax.rem(b + k % 4, 4)

    def device(place):
        return (place[0] * 4 + row, place[1] * 4 + col)

    def flipped(k):
        x = 2 * lax.rem(a0 + k // 8, 2) + lax.rem(a1 + k // 4 % 2, 2)
        y = 2 * lax.rem(b0 + k // 2 % 2, 2) + lax.rem(b1 + k % 2, 2)
        return x, y

    def load(k):
        x, y = ahead(k)
        at = pl.ds(pl.multiple_of((4 * x + y) * 128, 128), 128)
        return pltpu.make_async_copy(x_ref.at[:, :, at], xv.at[k], loads.at[k])

    def inward(half, k):
        return pltpu.make_async_remote_copy(
            src_ref=xp.at[half, k],
            dst_ref=xin.at[half, k],
            send_sem=send1.at[half, k],
            recv_sem=recv1.at[half, k],
            device_id=device(ahead(k)),
            device_id_type=MESH,
        )

    def outward(half, k):
        return pltpu.make_async_remote_copy(
            src_ref=ob.at[half, k],
            dst_ref=o_ref.at[me, half],
            send_sem=send2.at[half, k],
            recv_sem=recv2.at[half, k],
            device_id=device(flipped(k)),
            device_id_type=MESH,
        )

    along_z, along_y = (1, 2, 3), (4, 8, 12)
    straight = along_z + along_y
    order = straight + (6, 10, 14, 5, 9, 13, 7, 11, 15)
    barrier = pltpu.get_barrier_semaphore()
    for k in straight:
        pl.semaphore_signal(barrier, inc=1, device_id=device(ahead(k)), device_id_type=MESH)
    for k in order + (0,):
        load(k).start()
    lane = lax.broadcasted_iota(jnp.int32, (64, 128), 1)
    point = lax.broadcasted_iota(jnp.int32, (64, 128), 0)
    first_part = lane < 64

    def swapped(value):
        return pltpu.roll(value, 64, axis=1)

    def pack(k, into):
        real, imag = xv[k, 0], xv[k, 1]
        into[0, k] = jnp.where(first_part, real, swapped(imag))
        into[1, k] = jnp.where(first_part, swapped(real), imag)

    for k in straight:
        load(k).wait()
        pack(k, xp)
    pl.semaphore_wait(barrier, 6)
    for k in along_y:
        pl.semaphore_signal(told, inc=1, device_id=device(ahead(k)), device_id_type=MESH)
    for k in straight:
        inward(0, k).start()
    for k in order[6:]:
        load(k).wait()
        pack(k, xp)
    pl.semaphore_wait(told, 3)
    for k in order[6:]:
        inward(0, k).start()
    for k in straight:
        inward(1, k).start()
    for k in order[6:]:
        inward(1, k).start()
    load(0).wait()
    pack(0, xin)

    group = row * 4 + col
    px, py = group // 2, lax.rem(group, 2) * 4 + a
    zx, zy, zz = (chosen(point // w % 4, NODES) for w in (16, 4, 1))

    def lane_bit(index, width):
        return (index // width) % 2

    def as_f32(value):
        return value.astype(jnp.float32)

    ex, ey = as_f32(lane_bit(lane, 32)), as_f32(lane_bit(lane, 16))
    child, u8, u4 = lane_bit(lane, 64), lane_bit(lane, 8), lane_bit(lane, 4)
    u2, u1 = lane_bit(lane, 2), lane_bit(lane, 1)
    whole = weights()
    leading = whole.astype(jnp.bfloat16)
    mm[0:64, :] = leading
    mm[64:128, :] = (whole - leading.astype(jnp.float32)).astype(jnp.bfloat16)

    def speed(odd_x, odd_y, odd_z, scale):
        sine_x = sincos(as_f32(odd_x[0:8]) * scale)[1]
        sine_y = sincos(as_f32(odd_y[0:8]) * scale)[1]
        cosine_z = sincos(as_f32(odd_z[0:8]) * scale)[0]
        return 0.05 * (1.0 + 0.5 * sine_x * sine_y + 0.3 * cosine_z)

    def full(value):
        return jnp.full((64, 128), value, jnp.int32)

    def linear(odd_x, odd_y, odd_z):
        return as_f32(odd_x) * zx + as_f32(odd_y) * zy + as_f32(odd_z) * zz

    def prepare0(c, _):
        odd_x = 2 * (2 * px + child) + 1
        odd_y = full(2 * (2 * py + lax.rem(c, 2)) + 1)
        odd_z = 2 * (2 * (2 * b + c // 2) + u8) + 1
        kap0[c] = speed(odd_x, odd_y, odd_z, 1.0 / 32)
        lin0[c] = 0.5 + linear(odd_x, odd_y, odd_z)
        return 0

    lax.fori_loop(0, 4, prepare0, 0)

    def prepare1(c, _):
        cell_x, cell_y = 2 * px + c // 4 % 2, 2 * py + c // 2 % 2
        cell_z = 2 * (2 * b + c // 8) + u8
        parent = speed(full(2 * cell_x + 1), full(2 * cell_y + 1), 2 * cell_z + 1, 1.0 / 32)
        odd_x = full(2 * (2 * cell_x + lax.rem(c, 2)) + 1)
        odd_y, odd_z = 2 * (2 * cell_y + child) + 1, 2 * (2 * cell_z + u4) + 1
        kap2[c] = speed(odd_x, odd_y, odd_z, 1.0 / 64)
        dkap[c] = kap2[c] - parent
        lin2[c] = 2.0 * linear(odd_x, odd_y, odd_z)
        return 0

    lax.fori_loop(0, 16, prepare1, 0)
    for c in range(2):
        lin1[c] = 0.5 + linear(full(2 * c - 1), 2 * child - 1, 2 * u4 - 1)

    def square(width, at):
        p = width * at + (0.5 * width - 256.0)
        return p * p

    for n in range(4):
        squares[n] = square(32.0, 4.0 * ex + n + zx)
        squares[4 + n] = square(32.0, 4.0 * ey + n + zy)
    for n in range(2):
        squares[8 + n] = square(32.0, as_f32(8 * u2 + 4 * u1 + 2 * u4 + n) + zz)
        squares[10 + n] = square(64.0, 2.0 * ex + n + zx)
        squares[12 + n] = square(64.0, 2.0 * ey + n + zy)
        squares[14 + n] = square(64.0, as_f32(4 * u2 + 2 * u1 + n) + zz)

    def radius0(n, _):
        fx, fy = 2 * (n // 16) + n // 4 % 2, 2 * (n // 8 % 2) + n // 2 % 2
        r0[n] = jnp.sqrt(squares[fx] + squares[4 + fy] + squares[8 + n % 2])
        return 0

    def radius1(n, _):
        r1[n] = jnp.sqrt(squares[10 + n // 4] + squares[12 + n // 2 % 2] + squares[14 + n % 2])
        return 0

    lax.fori_loop(0, 32, radius0, 0)
    lax.fori_loop(0, 8, radius1, 0)
    r1[8] = jnp.sqrt(
        square(128.0, ex + zx) + square(128.0, ey + zy) + square(128.0, as_f32(2 * u2 + u1) + zz)
    )

    def tall(value):
        return jnp.broadcast_to(value[None], (8, 8, 128)).reshape(64, 128)

    def keep(table, at, turns):
        table[at, 0], table[at, 1] = sincos(turns)

    def fill(half):
        def fill0(n, _):
            for cy in range(2):
                c = half * 2 + cy
                keep(tab0, c * 32 + n, lin0[c] + tall(kap0[c]) * r0[n])
            return 0

        def fill1(step, _):
            first, n = step // 8, step % 8
            for dx in range(2):
                c = half * 8 + first * 2 + dx
                keep(tab1, c * 8 + n, lin1[dx] + tall(dkap[c]) * r1[n])
            return 0

        def fill2(step, _):
            c = half * 8 + step
            keep(tab2, c, lin2[c] + tall(kap2[c]) * r1[8])
            return 0

        lax.fori_loop(0, 32, fill0, 0)
        lax.fori_loop(0, 32, fill1, 0)
        lax.fori_loop(0, 8, fill2, 0)

    even = (lane // 16) % 4 * 16 + 8 * u2 + 4 * u1 + 2 * u4
    low4 = lane % 64 - 4 * u4

    def picked(value, index):
        return jnp.take_along_axis(value, index, axis=1, mode="promise_in_bounds")

    def arrange(half, k):
        x, y = lax.rem(a + 4 - k // 4, 4), lax.rem(b + 4 - k % 4, 4)
        n = (2 * (x % 2) + y % 2) * 8 + (2 * (x // 2) + y // 2) * 2
        got = xin[half, k]
        for bit in range(2):
            for part in range(2):
                xe[n + bit, part] = picked(got, even + (bit + 64 * part))

    def turn_and_sum(data, table, at):
        for n in range(8):
            real, imag = data(n)
            cosine, sine = table[at + n, 0], table[at + n, 1]
            out = (real * cosine - imag * sine, real * sine + imag * cosine)
            for part in range(2):
                high = out[part].astype(jnp.bfloat16)
                where = (pl.ds(64 * n, 64), pl.ds(128 * part, 128))
                wh[where] = high
                wl[where] = (out[part] - high.astype(jnp.float32)).astype(jnp.bfloat16)
        both = jnp.dot(mm[...], wh[...], preferred_element_type=jnp.float32)
        rest = jnp.dot(mm[0:64, :], wl[...], preferred_element_type=jnp.float32)
        total = both[0:64] + (both[64:128] + rest)
        return total[:, 0:128], total[:, 128:256]

    def box(half, _):
        arrange(half, 0)

        def arrive(k, _):
            inward(half, k).wait_recv()
            arrange(half, k)
            return 0

        lax.fori_loop(1, 16, arrive, 0)

        def first_y(across, _):
            cy = lax.rem(b0 + across, 2)

            def first_level(g, _):
                sums = turn_and_sum(
                    lambda n: (xe[g * 8 + n, 0], xe[g * 8 + n, 1]), tab0, (half * 2 + cy) * 32 + g * 8
                )
                for cx in range(2):
                    for bit in range(2):
                        for part in range(2):
                            v[cx * 8 + 2 * g + bit, part] = picked(
                                sums[part], low4 + (64 * cx + 4 * bit)
                            )
                return 0

            lax.fori_loop(0, 4, first_level, 0)

            def second_level(step, _):
                flips = (step + 1) % 4
                fx0, fx1 = flips // 2, flips % 2
                cx, dx = lax.rem(a0 + fx0, 2), lax.rem(a1 + fx1, 2)
                c = half * 8 + cx * 4 + cy * 2 + dx
                real, imag = turn_and_sum(lambda n: (v[cx * 8 + n, 0], v[cx * 8 + n, 1]), tab1, c * 8)
                cosine, sine = tab2[c, 0], tab2[c, 1]
                into = (real * cosine + imag * sine, imag * cosine - real * sine)
                for dy in range(2):
                    k = 8 * fx0 + 4 * fx1 + 2 * across + lax.rem(b1 + dy, 2)
                    if dy == 0:
                        ob[half, k] = jnp.where(first_part, into[0], swapped(into[1]))
                    else:
                        ob[half, k] = jnp.where(first_part, swapped(into[0]), into[1])

                    @pl.when(k > 0)
                    def _():
                        outward(half, k).start()

                return 0

            lax.fori_loop(0, 4, second_level, 0)
            return 0

        lax.fori_loop(0, 2, first_y, 0)
        return 0

    fill(0)
    fill(1)
    lax.fori_loop(0, 2, box, 0)
    own_out = [pltpu.make_async_copy(ob.at[h, 0], o_ref.at[me, h], own.at[h]) for h in range(2)]
    for copy in own_out:
        copy.start()

    def finish(k, _):
        for half in range(2):
            inward(half, k).wait_send()
            outward(half, k).wait_send()
            outward(half, k).wait_recv()
        return 0

    lax.fori_loop(1, 16, finish, 0)
    for copy in own_out:
        copy.wait()


def unpack(p_ref, o_ref, buf, sems):
    first_part = lax.broadcasted_iota(jnp.int32, (64, 128), 1) < 64
    copies = []
    for m in range(16):
        one, two = p_ref[m, 0], p_ref[m, 1]
        buf[m, 0] = jnp.where(first_part, one, pltpu.roll(two, 64, axis=1))
        buf[m, 1] = jnp.where(first_part, pltpu.roll(one, 64, axis=1), two)
        copy = pltpu.make_async_copy(buf.at[m], o_ref.at[:, :, pl.ds(128 * m, 128)], sems.at[m])
        copy.start()
        copies.append(copy)
    for copy in copies:
        copy.wait()


def local(coefficients):
    shape = coefficients.shape
    block = coefficients.reshape(shape[2:])
    f32, bf16 = jnp.float32, jnp.bfloat16
    packed = pl.pallas_call(
        kernel,
        out_shape=jax.ShapeDtypeStruct((16, 2, 64, 128), f32),
        in_specs=[pl.BlockSpec(memory_space=pl.ANY)],
        out_specs=pl.BlockSpec(memory_space=pl.ANY),
        scratch_shapes=[
            pltpu.VMEM((16, 2, 64, 128), f32),
            pltpu.VMEM((2, 16, 64, 128), f32),
            pltpu.VMEM((2, 16, 64, 128), f32),
            pltpu.VMEM((32, 2, 64, 128), f32),
            pltpu.VMEM((32, 64, 128), f32),
            pltpu.VMEM((9, 64, 128), f32),
            pltpu.VMEM((16, 64, 128), f32),
            pltpu.VMEM((128, 2, 64, 128), f32),
            pltpu.VMEM((128, 2, 64, 128), f32),
            pltpu.VMEM((16, 2, 64, 128), f32),
            pltpu.VMEM((16, 2, 64, 128), f32),
            pltpu.VMEM((512, 256), bf16),
            pltpu.VMEM((512, 256), bf16),
            pltpu.VMEM((2, 16, 64, 128), f32),
            pltpu.VMEM((128, 512), bf16),
            pltpu.VMEM((4, 64, 128), f32),
            pltpu.VMEM((2, 64, 128), f32),
            pltpu.VMEM((4, 8, 128), f32),
            pltpu.VMEM((16, 8, 128), f32),
            pltpu.VMEM((16, 8, 128), f32),
            pltpu.VMEM((16, 64, 128), f32),
            pltpu.SemaphoreType.DMA((2, 16)),
            pltpu.SemaphoreType.DMA((2, 16)),
            pltpu.SemaphoreType.DMA((2, 16)),
            pltpu.SemaphoreType.DMA((2, 16)),
            pltpu.SemaphoreType.DMA((16,)),
            pltpu.SemaphoreType.DMA((2,)),
            pltpu.SemaphoreType.REGULAR,
        ],
        compiler_params=pltpu.CompilerParams(
            collective_id=0, has_side_effects=True, vmem_limit_bytes=52 * 2**20
        ),
    )(block)
    out = pl.pallas_call(
        unpack,
        out_shape=jax.ShapeDtypeStruct(block.shape, f32),
        in_specs=[pl.BlockSpec(memory_space=pltpu.VMEM)],
        out_specs=pl.BlockSpec(memory_space=pl.ANY),
        scratch_shapes=[pltpu.VMEM((16, 2, 64, 128), f32), pltpu.SemaphoreType.DMA((16,))],
        compiler_params=pltpu.CompilerParams(vmem_limit_bytes=16 * 2**20),
    )(packed)
    return out.reshape(shape)


def solution(mesh):
    return jax.shard_map(
        local,
        mesh=mesh,
        in_specs=(P("bx", "by", None, None, None),),
        out_specs=P("bx", "by", None, None, None),
        check_vma=False,
    )
```

```python
import math

import jax
import jax.numpy as jnp
import numpy as np
from jax import lax
from jax.experimental import pallas as pl
from jax.experimental.pallas import tpu as pltpu
from jax.sharding import PartitionSpec as P

MESH = pl.DeviceIdType.MESH
NODES = [float(0.5 * np.cos((2 * k + 1) * np.pi / 8)) for k in range(4)]
SIN = [
    6.283182818516952,
    -41.341421395485554,
    81.59618379063296,
    -76.58009967534186,
    41.205391074799934,
    -12.271256275754906,
]
COS = [
    0.9999992215592304,
    -19.738982513358035,
    64.92872650603236,
    -85.27239557297074,
    58.79403136989473,
    -21.076769129657027,
]


def weights():
    row = lax.broadcasted_iota(jnp.int32, (64, 512), 0)
    column = lax.broadcasted_iota(jnp.int32, (64, 512), 1)

    def side(bit, t, s):
        at = 0.5 * (bit.astype(jnp.float32) - 0.5) + 0.5 * chosen(s, NODES)
        out = chosen(
            t, [1.0 / math.prod(NODES[t] - z for z in NODES if z != NODES[t]) for t in range(4)]
        )
        for k in range(4):
            out = jnp.where(t == k, out, out * (at - NODES[k]))
        return out

    first = side(column // 256, row // 16, column // 16 % 4)
    second = side(column // 128 % 2, row // 4 % 4, column // 4 % 4)
    return first * second * side(column // 64 % 2, row % 4, column % 4)


def chosen(digit, values):
    out = jnp.full(digit.shape, values[3], jnp.float32)
    for k in range(3):
        out = jnp.where(digit == k, values[k], out)
    return out


def sincos(turns):
    turns = turns - jnp.round(turns)
    square = turns * turns
    sine = jnp.full_like(turns, SIN[-1])
    for c in SIN[-2::-1]:
        sine = sine * square + c
    cosine = jnp.full_like(turns, COS[-1])
    for c in COS[-2::-1]:
        cosine = cosine * square + c
    return cosine, sine * turns


def kernel(
    x_ref, o_ref, xv, xp, xin, xe, r0, r1, squares, tab0, tab1, tab2, v, wh, wl, ob, mm, lin0, lin1,
    kap0, dkap, kap2, lin2, send1, recv1, send2, recv2, loads, own,
    told,
):
    bx, by = lax.axis_index("bx"), lax.axis_index("by")
    a, b = bx // 4, by // 4
    row, col = lax.rem(bx, 4), lax.rem(by, 4)
    a0, a1, b0, b1 = a // 2, lax.rem(a, 2), b // 2, lax.rem(b, 2)
    me = 4 * a + b

    def ahead(k):
        return lax.rem(a + k // 4, 4), lax.rem(b + k % 4, 4)

    def device(place):
        return (place[0] * 4 + row, place[1] * 4 + col)

    def flipped(k):
        x = 2 * lax.rem(a0 + k // 8, 2) + lax.rem(a1 + k // 4 % 2, 2)
        y = 2 * lax.rem(b0 + k // 2 % 2, 2) + lax.rem(b1 + k % 2, 2)
        return x, y

    def load(k):
        x, y = ahead(k)
        at = pl.ds(pl.multiple_of((4 * x + y) * 128, 128), 128)
        return pltpu.make_async_copy(x_ref.at[:, :, at], xv.at[k], loads.at[k])

    def inward(half, k):
        return pltpu.make_async_remote_copy(
            src_ref=xp.at[half, k],
            dst_ref=xin.at[half, k],
            send_sem=send1.at[half, k],
            recv_sem=recv1.at[half, k],
            device_id=device(ahead(k)),
            device_id_type=MESH,
        )

    def outward(half, k):
        return pltpu.make_async_remote_copy(
            src_ref=ob.at[half, k],
            dst_ref=o_ref.at[me, half],
            send_sem=send2.at[half, k],
            recv_sem=recv2.at[half, k],
            device_id=device(flipped(k)),
            device_id_type=MESH,
        )

    along_z, along_y = (1, 2, 3), (4, 8, 12)
    straight = along_z + along_y
    order = straight + (6, 10, 14, 5, 9, 13, 7, 11, 15)
    barrier = pltpu.get_barrier_semaphore()
    for k in straight:
        pl.semaphore_signal(barrier, inc=1, device_id=device(ahead(k)), device_id_type=MESH)
    for k in order + (0,):
        load(k).start()
    lane = lax.broadcasted_iota(jnp.int32, (64, 128), 1)
    point = lax.broadcasted_iota(jnp.int32, (64, 128), 0)
    first_part = lane < 64

    def swapped(value):
        return pltpu.roll(value, 64, axis=1)

    def pack(k, into):
        real, imag = xv[k, 0], xv[k, 1]
        into[0, k] = jnp.where(first_part, real, swapped(imag))
        into[1, k] = jnp.where(first_part, swapped(real), imag)

    for k in straight:
        load(k).wait()
        pack(k, xp)
    pl.semaphore_wait(barrier, 6)
    for k in along_y:
        pl.semaphore_signal(told, inc=1, device_id=device(ahead(k)), device_id_type=MESH)
    for k in straight:
        inward(0, k).start()
    for k in order[6:]:
        load(k).wait()
        pack(k, xp)
    pl.semaphore_wait(told, 3)
    for k in order[6:]:
        inward(0, k).start()
    load(0).wait()
    pack(0, xin)

    group = row * 4 + col
    px, py = group // 2, lax.rem(group, 2) * 4 + a
    zx, zy, zz = (chosen(point // w % 4, NODES) for w in (16, 4, 1))

    def lane_bit(index, width):
        return (index // width) % 2

    def as_f32(value):
        return value.astype(jnp.float32)

    ex, ey = as_f32(lane_bit(lane, 32)), as_f32(lane_bit(lane, 16))
    child, u8, u4 = lane_bit(lane, 64), lane_bit(lane, 8), lane_bit(lane, 4)
    u2, u1 = lane_bit(lane, 2), lane_bit(lane, 1)
    whole = weights()
    leading = whole.astype(jnp.bfloat16)
    mm[0:64, :] = leading
    mm[64:128, :] = (whole - leading.astype(jnp.float32)).astype(jnp.bfloat16)

    def speed(odd_x, odd_y, odd_z, scale):
        sine_x = sincos(as_f32(odd_x[0:8]) * scale)[1]
        sine_y = sincos(as_f32(odd_y[0:8]) * scale)[1]
        cosine_z = sincos(as_f32(odd_z[0:8]) * scale)[0]
        return 0.05 * (1.0 + 0.5 * sine_x * sine_y + 0.3 * cosine_z)

    def full(value):
        return jnp.full((64, 128), value, jnp.int32)

    def linear(odd_x, odd_y, odd_z):
        return as_f32(odd_x) * zx + as_f32(odd_y) * zy + as_f32(odd_z) * zz

    def prepare0(c, _):
        odd_x = 2 * (2 * px + child) + 1
        odd_y = full(2 * (2 * py + lax.rem(c, 2)) + 1)
        odd_z = 2 * (2 * (2 * b + c // 2) + u8) + 1
        kap0[c] = speed(odd_x, odd_y, odd_z, 1.0 / 32)
        lin0[c] = 0.5 + linear(odd_x, odd_y, odd_z)
        return 0

    lax.fori_loop(0, 4, prepare0, 0)

    def prepare1(c, _):
        cell_x, cell_y = 2 * px + c // 4 % 2, 2 * py + c // 2 % 2
        cell_z = 2 * (2 * b + c // 8) + u8
        parent = speed(full(2 * cell_x + 1), full(2 * cell_y + 1), 2 * cell_z + 1, 1.0 / 32)
        odd_x = full(2 * (2 * cell_x + lax.rem(c, 2)) + 1)
        odd_y, odd_z = 2 * (2 * cell_y + child) + 1, 2 * (2 * cell_z + u4) + 1
        kap2[c] = speed(odd_x, odd_y, odd_z, 1.0 / 64)
        dkap[c] = kap2[c] - parent
        lin2[c] = 2.0 * linear(odd_x, odd_y, odd_z)
        return 0

    lax.fori_loop(0, 16, prepare1, 0)
    for c in range(2):
        lin1[c] = 0.5 + linear(full(2 * c - 1), 2 * child - 1, 2 * u4 - 1)

    def square(width, at):
        p = width * at + (0.5 * width - 256.0)
        return p * p

    for n in range(4):
        squares[n] = square(32.0, 4.0 * ex + n + zx)
        squares[4 + n] = square(32.0, 4.0 * ey + n + zy)
    for n in range(2):
        squares[8 + n] = square(32.0, as_f32(8 * u2 + 4 * u1 + 2 * u4 + n) + zz)
        squares[10 + n] = square(64.0, 2.0 * ex + n + zx)
        squares[12 + n] = square(64.0, 2.0 * ey + n + zy)
        squares[14 + n] = square(64.0, as_f32(4 * u2 + 2 * u1 + n) + zz)

    def radius0(n, _):
        fx, fy = 2 * (n // 16) + n // 4 % 2, 2 * (n // 8 % 2) + n // 2 % 2
        r0[n] = jnp.sqrt(squares[fx] + squares[4 + fy] + squares[8 + n % 2])
        return 0

    def radius1(n, _):
        r1[n] = jnp.sqrt(squares[10 + n // 4] + squares[12 + n // 2 % 2] + squares[14 + n % 2])
        return 0

    lax.fori_loop(0, 32, radius0, 0)
    lax.fori_loop(0, 8, radius1, 0)
    r1[8] = jnp.sqrt(
        square(128.0, ex + zx) + square(128.0, ey + zy) + square(128.0, as_f32(2 * u2 + u1) + zz)
    )

    for k in straight:
        inward(1, k).start()
    for k in order[6:]:
        inward(1, k).start()

    def tall(value):
        return jnp.broadcast_to(value[None], (8, 8, 128)).reshape(64, 128)

    def keep(table, at, turns):
        table[at, 0], table[at, 1] = sincos(turns)

    def fill(half):
        def fill0(n, _):
            for cy in range(2):
                c = half * 2 + cy
                keep(tab0, c * 32 + n, lin0[c] + tall(kap0[c]) * r0[n])
            return 0

        def fill1(step, _):
            first, n = step // 8, step % 8
            for dx in range(2):
                c = half * 8 + first * 2 + dx
                keep(tab1, c * 8 + n, lin1[dx] + tall(dkap[c]) * r1[n])
            return 0

        def fill2(step, _):
            c = half * 8 + step
            keep(tab2, c, lin2[c] + tall(kap2[c]) * r1[8])
            return 0

        lax.fori_loop(0, 32, fill0, 0)
        lax.fori_loop(0, 32, fill1, 0)
        lax.fori_loop(0, 8, fill2, 0)

    even = (lane // 16) % 4 * 16 + 8 * u2 + 4 * u1 + 2 * u4
    low4 = lane % 64 - 4 * u4

    def picked(value, index):
        return jnp.take_along_axis(value, index, axis=1, mode="promise_in_bounds")

    def arrange(half, k):
        x, y = lax.rem(a + 4 - k // 4, 4), lax.rem(b + 4 - k % 4, 4)
        n = (2 * (x % 2) + y % 2) * 8 + (2 * (x // 2) + y // 2) * 2
        got = xin[half, k]
        for bit in range(2):
            for part in range(2):
                xe[n + bit, part] = picked(got, even + (bit + 64 * part))

    def turn_and_sum(data, table, at):
        for n in range(8):
            real, imag = data(n)
            cosine, sine = table[at + n, 0], table[at + n, 1]
            out = (real * cosine - imag * sine, real * sine + imag * cosine)
            for part in range(2):
                high = out[part].astype(jnp.bfloat16)
                where = (pl.ds(64 * n, 64), pl.ds(128 * part, 128))
                wh[where] = high
                wl[where] = (out[part] - high.astype(jnp.float32)).astype(jnp.bfloat16)
        both = jnp.dot(mm[...], wh[...], preferred_element_type=jnp.float32)
        rest = jnp.dot(mm[0:64, :], wl[...], preferred_element_type=jnp.float32)
        total = both[0:64] + (both[64:128] + rest)
        return total[:, 0:128], total[:, 128:256]

    def box(half, _):
        arrange(half, 0)

        def arrive(k, _):
            inward(half, k).wait_recv()
            arrange(half, k)
            return 0

        lax.fori_loop(1, 16, arrive, 0)

        def first_y(across, _):
            cy = lax.rem(b0 + across, 2)

            def first_level(g, _):
                sums = turn_and_sum(
                    lambda n: (xe[g * 8 + n, 0], xe[g * 8 + n, 1]), tab0, (half * 2 + cy) * 32 + g * 8
                )
                for cx in range(2):
                    for bit in range(2):
                        for part in range(2):
                            v[cx * 8 + 2 * g + bit, part] = picked(
                                sums[part], low4 + (64 * cx + 4 * bit)
                            )
                return 0

            lax.fori_loop(0, 4, first_level, 0)

            def second_level(step, _):
                flips = (step + 1) % 4
                fx0, fx1 = flips // 2, flips % 2
                cx, dx = lax.rem(a0 + fx0, 2), lax.rem(a1 + fx1, 2)
                c = half * 8 + cx * 4 + cy * 2 + dx
                real, imag = turn_and_sum(lambda n: (v[cx * 8 + n, 0], v[cx * 8 + n, 1]), tab1, c * 8)
                cosine, sine = tab2[c, 0], tab2[c, 1]
                into = (real * cosine + imag * sine, imag * cosine - real * sine)
                for dy in range(2):
                    k = 8 * fx0 + 4 * fx1 + 2 * across + lax.rem(b1 + dy, 2)
                    if dy == 0:
                        ob[half, k] = jnp.where(first_part, into[0], swapped(into[1]))
                    else:
                        ob[half, k] = jnp.where(first_part, swapped(into[0]), into[1])

                    @pl.when(k > 0)
                    def _():
                        outward(half, k).start()

                return 0

            lax.fori_loop(0, 4, second_level, 0)
            return 0

        lax.fori_loop(0, 2, first_y, 0)
        return 0

    fill(0)
    fill(1)
    lax.fori_loop(0, 2, box, 0)
    own_out = [pltpu.make_async_copy(ob.at[h, 0], o_ref.at[me, h], own.at[h]) for h in range(2)]
    for copy in own_out:
        copy.start()

    def finish(k, _):
        for half in range(2):
            inward(half, k).wait_send()
            outward(half, k).wait_send()
            outward(half, k).wait_recv()
        return 0

    lax.fori_loop(1, 16, finish, 0)
    for copy in own_out:
        copy.wait()


def unpack(p_ref, o_ref, buf, sems):
    first_part = lax.broadcasted_iota(jnp.int32, (64, 128), 1) < 64
    copies = []
    for m in range(16):
        one, two = p_ref[m, 0], p_ref[m, 1]
        buf[m, 0] = jnp.where(first_part, one, pltpu.roll(two, 64, axis=1))
        buf[m, 1] = jnp.where(first_part, pltpu.roll(one, 64, axis=1), two)
        copy = pltpu.make_async_copy(buf.at[m], o_ref.at[:, :, pl.ds(128 * m, 128)], sems.at[m])
        copy.start()
        copies.append(copy)
    for copy in copies:
        copy.wait()


def local(coefficients):
    shape = coefficients.shape
    block = coefficients.reshape(shape[2:])
    f32, bf16 = jnp.float32, jnp.bfloat16
    packed = pl.pallas_call(
        kernel,
        out_shape=jax.ShapeDtypeStruct((16, 2, 64, 128), f32),
        in_specs=[pl.BlockSpec(memory_space=pl.ANY)],
        out_specs=pl.BlockSpec(memory_space=pl.ANY),
        scratch_shapes=[
            pltpu.VMEM((16, 2, 64, 128), f32),
            pltpu.VMEM((2, 16, 64, 128), f32),
            pltpu.VMEM((2, 16, 64, 128), f32),
            pltpu.VMEM((32, 2, 64, 128), f32),
            pltpu.VMEM((32, 64, 128), f32),
            pltpu.VMEM((9, 64, 128), f32),
            pltpu.VMEM((16, 64, 128), f32),
            pltpu.VMEM((128, 2, 64, 128), f32),
            pltpu.VMEM((128, 2, 64, 128), f32),
            pltpu.VMEM((16, 2, 64, 128), f32),
            pltpu.VMEM((16, 2, 64, 128), f32),
            pltpu.VMEM((512, 256), bf16),
            pltpu.VMEM((512, 256), bf16),
            pltpu.VMEM((2, 16, 64, 128), f32),
            pltpu.VMEM((128, 512), bf16),
            pltpu.VMEM((4, 64, 128), f32),
            pltpu.VMEM((2, 64, 128), f32),
            pltpu.VMEM((4, 8, 128), f32),
            pltpu.VMEM((16, 8, 128), f32),
            pltpu.VMEM((16, 8, 128), f32),
            pltpu.VMEM((16, 64, 128), f32),
            pltpu.SemaphoreType.DMA((2, 16)),
            pltpu.SemaphoreType.DMA((2, 16)),
            pltpu.SemaphoreType.DMA((2, 16)),
            pltpu.SemaphoreType.DMA((2, 16)),
            pltpu.SemaphoreType.DMA((16,)),
            pltpu.SemaphoreType.DMA((2,)),
            pltpu.SemaphoreType.REGULAR,
        ],
        compiler_params=pltpu.CompilerParams(
            collective_id=0, has_side_effects=True, vmem_limit_bytes=52 * 2**20
        ),
    )(block)
    out = pl.pallas_call(
        unpack,
        out_shape=jax.ShapeDtypeStruct(block.shape, f32),
        in_specs=[pl.BlockSpec(memory_space=pltpu.VMEM)],
        out_specs=pl.BlockSpec(memory_space=pl.ANY),
        scratch_shapes=[pltpu.VMEM((16, 2, 64, 128), f32), pltpu.SemaphoreType.DMA((16,))],
        compiler_params=pltpu.CompilerParams(vmem_limit_bytes=16 * 2**20),
    )(packed)
    return out.reshape(shape)


def solution(mesh):
    return jax.shard_map(
        local,
        mesh=mesh,
        in_specs=(P("bx", "by", None, None, None),),
        out_specs=P("bx", "by", None, None, None),
        check_vma=False,
    )
```
